768 devices in a mesh: blk: 192 (over z, y_hi, x, core), group: 4 (over y_lo).
Axes of the slice: x: 4, y: 8 (y_hi: 2, y_lo: 4; y = y_hi * 4 + y_lo), z: 12, core: 2. Of those that a mesh axis runs over, the one named last changes fastest.
Arguments:
- images: bfloat16 [196608, 768], P('blk'), may hold values from -0.5 to 0.5
- captions: bfloat16 [196608, 768], P(('blk', 'group')), may hold values from -0.5 to 0.5
- pairing: int32 [192, 1024], P('blk', 'group'), may hold values from 0 to 1023, each once within a row
- logit_scale: float32 [1], replicated, may hold values from 5 to 15
- logit_bias: float32 [1], replicated, may hold values from -4 to -2
Outputs:
- image_grad: float32 [196608, 768], P(('blk', 'group'))
- caption_grad: float32 [196608, 768], P(('blk', 'group'))
- loss_rows: float32 [196608], P(('blk', 'group'))
The draws below stay inside these ranges and needn't reach their ends.
Inputs may be any that keep to these rules, and one draw needn't show every extreme that they name: Each row of pairing is a permutation of 0 .. 1023.
All inputs are finite; a program needn't handle non-finite values.
Results may differ from the reference program's by a relative error of at most 0.0043.
Values may be sent and summed in bfloat16 or wider, within the bound.
No kernel may reach another device: no remote copies, remote signals or barrier semaphores. Data moves between devices by JAX's collectives and lax.ppermute only.
A program may use at most 32 MiB of HBM per device.

```python
import jax
import jax.numpy as jnp
from jax import lax

D = 768
TOK_DEV = 256
STEPS = 4
IMG_BLK = 1024
IMAGES = 196608
CAPTIONS = 196608
N_BLK = 192


def block_levels(own_key, dims, cuts, least, largest):
    gain, own = 1.0, jax.random.fold_in(own_key, 6)
    for axis_at, parts in cuts:
        draws = jnp.exp(jax.random.uniform(jax.random.fold_in(own, axis_at), (parts,), jnp.float32, least / len(cuts), largest / len(cuts)))
        gain = gain * jnp.repeat(draws, dims[axis_at] // parts).reshape([-1 if axis == axis_at else 1 for axis in range(len(dims))])
    return gain


def gaussian(rng, dims, deviation, reach, cuts=(), dtype=jnp.bfloat16):
    entries = deviation * jax.random.normal(rng, dims, jnp.float32)
    if cuts:
        entries = entries * block_levels(rng, dims, cuts, -0.22, 0.18)
    return jnp.clip(entries, -reach, reach).astype(dtype)


def setup_inputs(seed: int = 0) -> dict:
    streams_of = jax.random.split(jax.random.key(seed), 6)
    images = gaussian(streams_of[0], (IMAGES, D), 0.036, 0.5, ((0, 192),))
    captions = gaussian(streams_of[1], (CAPTIONS, D), 0.036, 0.5, ((0, 768),))
    pairing = jax.vmap(lambda own: jax.random.permutation(own, IMG_BLK))(jax.random.split(streams_of[2], N_BLK)).reshape((N_BLK, IMG_BLK)).astype(jnp.int32)
    logit_scale = jnp.clip(jax.random.uniform(streams_of[3], (1,), jnp.float32, 5.0, 15.0), 5.0, 15.0)
    logit_bias = jnp.clip(jax.random.uniform(streams_of[4], (1,), jnp.float32, -4.0, -2.0), -4.0, -2.0)
    return dict(images=images, captions=captions, pairing=pairing, logit_scale=logit_scale, logit_bias=logit_bias)


def unit_rows(values):
    as_float = values.astype(jnp.float32)
    inverse = lax.rsqrt(lax.optimization_barrier(jnp.sum(as_float * as_float, axis=-1, keepdims=True)) + 1e-06)
    return (as_float * inverse, inverse)

def norm_back(unit, inverse, upstream):
    return inverse * (upstream - unit * lax.optimization_barrier(jnp.sum(unit * upstream, axis=-1, keepdims=True)))

def reference(images, captions, pairing, logit_scale, logit_bias):
    image_unit, image_inv = unit_rows(images)
    caption_unit, caption_inv = unit_rows(captions)
    image_blocks = lax.optimization_barrier(image_unit.astype(jnp.bfloat16)).astype(jnp.float32).reshape(N_BLK, IMG_BLK, D)
    caption_blocks = lax.optimization_barrier(caption_unit.astype(jnp.bfloat16)).astype(jnp.float32).reshape(N_BLK, IMG_BLK, D)
    positive = pairing[:, None, :] == lax.broadcasted_iota(jnp.int32, (1, IMG_BLK, 1), 1)
    first_signs = jnp.where(positive, jnp.float32(1.0), jnp.float32(-1.0)).astype(jnp.float32)
    other_signs = -jnp.ones((N_BLK, IMG_BLK, IMG_BLK), jnp.float32)
    scale_value = logit_scale[0]
    bias_value = logit_bias[0]
    image_upstream = jnp.zeros((N_BLK, IMG_BLK, D), jnp.float32)
    caption_upstream = jnp.zeros((N_BLK, IMG_BLK, D), jnp.float32)
    loss_sum = jnp.zeros((N_BLK, IMG_BLK), jnp.float32)
    for offset in range(STEPS):
        visiting = jnp.roll(caption_blocks, offset, axis=0)
        label_signs = first_signs if offset == 0 else other_signs
        logits = scale_value * jnp.einsum('bid,bjd->bij', image_blocks, visiting) + bias_value
        loss_sum = loss_sum + lax.optimization_barrier(jnp.sum(jax.nn.softplus(-label_signs * logits), axis=2))
        pair_slope = -label_signs * jax.nn.sigmoid(-label_signs * logits)
        pair_slope = lax.optimization_barrier(pair_slope.astype(jnp.bfloat16)).astype(jnp.float32)
        image_upstream = image_upstream + scale_value * jnp.einsum('bij,bjd->bid', pair_slope, visiting)
        caption_term = scale_value * jnp.einsum('bij,bid->bjd', pair_slope, image_blocks)
        caption_upstream = caption_upstream + jnp.roll(caption_term, -offset, axis=0)
    image_grad = norm_back(image_unit, image_inv, image_upstream.reshape(N_BLK * IMG_BLK, D))
    caption_grad = norm_back(caption_unit, caption_inv, caption_upstream.reshape(N_BLK * IMG_BLK, D))
    loss_rows = loss_sum.reshape(N_BLK * IMG_BLK) / (STEPS * TOK_DEV)
    return (image_grad, caption_grad, loss_rows)
```

```python
import jax
import jax.numpy as jnp
from jax import lax
from jax.sharding import PartitionSpec as P

TOK_DEV = 256
STEPS = 4
AXES = ("blk", "group")
ROW = 8
PAD = 16


def unit_rows(values):
    as_float = values.astype(jnp.float32)
    inverse = lax.rsqrt(jnp.sum(as_float * as_float, axis=-1, keepdims=True) + 1e-06)
    return (as_float * inverse, inverse)


def norm_back(unit, inverse, upstream):
    return inverse * (upstream - unit * jnp.sum(unit * upstream, axis=-1, keepdims=True))


def ring_routes(n_blk, n_group):
    forward = []
    for b in range(n_blk):
        for g in range(n_group):
            t = (b + 1) % n_blk
            lane = n_group - 1 - g if t // ROW != b // ROW else g
            forward.append((b * n_group + g, t * n_group + lane))
    return forward, [(t, s) for s, t in forward]


def group_routes(n_blk, n_group, pairs):
    return [(b * n_group + s, b * n_group + t) for b in range(n_blk) for s, t in pairs]


def pair_terms(image_bf, visiting, scale_value, bias_value, label_signs):
    logits = (
        scale_value
        * lax.dot_general(
            image_bf, visiting, (((1,), (1,)), ((), ())), preferred_element_type=jnp.float32
        )
        + bias_value
    )
    signed = -label_signs * logits
    loss_part = jnp.sum(jax.nn.softplus(signed), axis=1)
    pair_slope = (-label_signs * jax.nn.sigmoid(signed)).astype(jnp.bfloat16)
    caption_term = scale_value * lax.dot_general(
        pair_slope, image_bf, (((0,), (0,)), ((), ())), preferred_element_type=jnp.float32
    )
    return loss_part, pair_slope, caption_term


def body(images, captions, pairing, logit_scale, logit_bias):
    n_blk, n_group = lax.axis_size("blk"), lax.axis_size("group")
    forward, backward = ring_routes(n_blk, n_group)
    lane = lax.axis_index("group")

    def send(block, route):
        return lax.ppermute(block, AXES, route)

    caption_unit, caption_inv = unit_rows(captions)
    caption_bf = caption_unit.astype(jnp.bfloat16)
    visits = [caption_bf]
    for _ in range(1, STEPS):
        visits.append(send(visits[-1], forward))
    image_unit, image_inv = unit_rows(images)
    image_bf = image_unit.astype(jnp.bfloat16)
    scale_value = logit_scale[0]
    bias_value = logit_bias[0]
    row_count = image_bf.shape[0]
    col_count = caption_bf.shape[0]
    positive = pairing[0][None, :] == lax.broadcasted_iota(jnp.int32, (row_count, col_count), 0)
    signs = [jnp.where(positive, 1.0, -1.0).astype(jnp.float32)] + [jnp.float32(-1.0)] * 3
    losses, slopes, caption_terms = zip(
        *[pair_terms(image_bf, v, scale_value, bias_value, s) for v, s in zip(visits, signs)]
    )
    carried = caption_terms[3].astype(jnp.bfloat16)
    carried = send(carried, backward)
    carried = (carried.astype(jnp.float32) + caption_terms[2]).astype(jnp.bfloat16)
    carried = send(carried, backward)
    carried = (carried.astype(jnp.float32) + caption_terms[1]).astype(jnp.bfloat16)
    carried = send(carried, backward)
    caption_upstream = carried.astype(jnp.float32) + caption_terms[0]

    loss_sum = losses[0] + losses[1] + losses[2] + losses[3]
    image_term = scale_value * sum(
        jnp.dot(s, v, preferred_element_type=jnp.float32) for s, v in zip(slopes, visits)
    )
    share_rows = row_count // n_group
    loss_hi = loss_sum.astype(jnp.bfloat16)
    loss_lo = (loss_sum - loss_hi.astype(jnp.float32)).astype(jnp.bfloat16)
    tail = jnp.concatenate([loss_hi.reshape(n_group, 1, share_rows), loss_lo.reshape(n_group, 1, share_rows)], axis=1)
    tail = jnp.pad(tail, ((0, 0), (0, PAD - 2), (0, image_term.shape[1] - share_rows)))
    parts = jnp.concatenate(
        [image_term.astype(jnp.bfloat16).reshape(n_group, share_rows, -1), tail], axis=1
    )

    def part(table):
        at = jnp.asarray(table, jnp.int32)[lane]
        return lax.dynamic_index_in_dim(parts, at, 0, keepdims=False)

    def add(a, b):
        return (a.astype(jnp.float32) + b.astype(jnp.float32)).astype(jnp.bfloat16)

    carry = send(part([3, 0, 0, 0]), group_routes(n_blk, n_group, [(0, 1), (3, 2)]))
    near = send(part([1, 0, 3, 2]), group_routes(n_blk, n_group, [(0, 1), (1, 0), (2, 3), (3, 2)]))
    middle = send(part([0, 2, 1, 0]), group_routes(n_blk, n_group, [(1, 2), (2, 1)]))
    far = send(
        add(part([2, 3, 0, 1]), carry), group_routes(n_blk, n_group, [(0, 2), (1, 3), (2, 0), (3, 1)])
    )
    pieces = [part([0, 1, 2, 3]), near, middle, far]
    share = sum(p.astype(jnp.float32) for p in pieces)
    image_share = share[:share_rows]
    loss_share = share[share_rows, :share_rows] + share[share_rows + 1, :share_rows]
    start = lane * share_rows
    own_unit = lax.dynamic_slice_in_dim(image_unit, start, share_rows, 0)
    own_inv = lax.dynamic_slice_in_dim(image_inv, start, share_rows, 0)
    image_grad = norm_back(own_unit, own_inv, image_share)
    caption_grad = norm_back(caption_unit, caption_inv, caption_upstream)
    loss_rows = loss_share / (STEPS * TOK_DEV)
    return (image_grad, caption_grad, loss_rows)


def solution(mesh):
    in_specs = (P("blk", None), P(("blk", "group"), None), P("blk", "group"), P(), P())
    out_specs = (P(("blk", "group"), None), P(("blk", "group"), None), P(("blk", "group")))
    return jax.shard_map(body, mesh=mesh, in_specs=in_specs, out_specs=out_specs, check_vma=False)
```

```python
import jax
import jax.numpy as jnp
from jax import lax
from jax.experimental import pallas as pl
from jax.experimental.pallas import tpu as pltpu
from jax.sharding import PartitionSpec as P

TOK_DEV = 256
STEPS = 4
AXES = ("blk", "group")
ROW = 8
PAD = 16
VMEM_BYTES = 16 * 1024 * 1024
NT = (((1,), (1,)), ((), ()))


def vmem():
    return pl.BlockSpec(memory_space=pltpu.VMEM)


def smem():
    return pl.BlockSpec(memory_space=pltpu.SMEM)


def anywhere():
    return pl.BlockSpec(memory_space=pl.ANY)


def call(kernel, outs, ins, flops, name, args, scratch=()):
    return pl.pallas_call(
        kernel,
        out_shape=outs,
        in_specs=ins,
        out_specs=jax.tree.map(lambda _: vmem(), outs),
        scratch_shapes=scratch,
        compiler_params=pltpu.CompilerParams(vmem_limit_bytes=VMEM_BYTES),
        cost_estimate=pl.CostEstimate(
            flops=flops, bytes_accessed=4 * 1024 * 1024, transcendentals=0
        ),
        name=name,
    )(*args)


def shape(dims, dtype):
    return jax.ShapeDtypeStruct(dims, dtype)


def unit_rows(values):
    as_float = values.astype(jnp.float32)
    inverse = lax.rsqrt(jnp.sum(as_float * as_float, axis=-1, keepdims=True) + 1e-06)
    return as_float * inverse, inverse


def norm_kernel(captions, out):
    out[...] = unit_rows(captions[...])[0].astype(jnp.bfloat16)


def pair_chunk(visiting, image, scale, bias, positive):
    logits = (
        scale * lax.dot_general(visiting, image, NT, preferred_element_type=jnp.float32) + bias
    )
    signed = logits if positive is None else jnp.where(positive, -logits, logits)
    small = jnp.exp(-jnp.abs(signed))
    whole = 1.0 + small
    inverse = 1.0 / whole
    log1p = jnp.log(whole) + (small - (whole - 1.0)) * inverse
    loss = jnp.sum(jnp.maximum(signed, 0.0) + log1p, axis=0, keepdims=True)
    slope = jnp.where(signed >= 0.0, inverse, small * inverse)
    if positive is not None:
        slope = jnp.where(positive, -slope, slope)
    return loss, slope


def first_kernel(images, visiting, pairing, scale, bias, image_bf, loss, slopes, grad, total):
    n, rows = TOK_DEV, image_bf.shape[0]
    held = visiting[...]
    for c in range(rows // n):
        at = slice(c * n, (c + 1) * n)
        image = unit_rows(images[at, :])[0].astype(jnp.bfloat16)
        image_bf[at, :] = image
        positive = pairing[...] == c * n + lax.broadcasted_iota(jnp.int32, (n, n), 1)
        part, slope = pair_chunk(held, image, scale[0], bias[0], positive)
        loss[:, at] = part
        slopes[at, :] = slope.T.astype(jnp.bfloat16)
        term = jnp.dot(slope.astype(jnp.bfloat16), image, preferred_element_type=jnp.float32)
        if c == 0:
            total[...] = term
        elif c < rows // n - 1:
            total[...] += term
        else:
            grad[...] = scale[0] * (total[...] + term)


def next_kernel(place, image_bf, f2, f3, before, scale, bias, loss, slopes, grad, held_out, total):
    n, rows = TOK_DEV, image_bf.shape[0]
    held = jnp.where(place[0] == 2, f2[...], f3[...])
    held_out[...] = held
    for c in range(rows // n):
        at = slice(c * n, (c + 1) * n)
        image = image_bf[at, :]
        part, slope = pair_chunk(held, image, scale[0], bias[0], None)
        loss[:, at] = before[:, at] + part
        slopes[at, :] = slope.T.astype(jnp.bfloat16)
        term = jnp.dot(slope.astype(jnp.bfloat16), image, preferred_element_type=jnp.float32)
        if c == 0:
            total[...] = term
        elif c < rows // n - 1:
            total[...] += term
        else:
            grad[...] = (scale[0] * (total[...] + term)).astype(grad.dtype)


def last_kernel(
    lane, place, scale, bias, image_bf, v0, f1, f2, vc, y1, y2, f5, before, s0_in, sc_in,
    across, near, far, own, grad_a, grad_b, to_swap,
    s0, sa, sb, sc, va, vb, total_a, total_b, loss, sems,
):
    n, rows, g = TOK_DEV, image_bf.shape[0], lane[0]
    copies = [pltpu.make_async_copy(s0_in, s0, sems.at[0]), pltpu.make_async_copy(sc_in, sc, sems.at[1])]
    for copy in copies:
        copy.start()
    first, second, third = place[0] == 0, place[0] == 1, place[0] == 2
    for held, choices in (
        (va, ((first, y1), (~first, f1))),
        (vb, ((first, f5), (second, y1), (third, y2), (place[0] > 2, f2))),
    ):
        for chosen, source in choices:

            @pl.when(chosen)
            def _():
                held[...] = source[...]

    for c in range(rows // n):
        at = slice(c * n, (c + 1) * n)
        image = image_bf[at, :]
        sums = before[:, at]
        for v, s, total in ((va, sa, total_a), (vb, sb, total_b)):
            part, slope = pair_chunk(v[...], image, scale[0], bias[0], None)
            sums = sums + part
            s[at, :] = slope.T.astype(jnp.bfloat16)
            term = jnp.dot(slope.astype(jnp.bfloat16), image, preferred_element_type=jnp.float32)
            if c == 0:
                total[...] = term
            else:
                total[...] += term
        loss[:, at] = sums
    grad_a[...] = (scale[0] * total_a[...]).astype(jnp.bfloat16)
    grad_b[...] = (scale[0] * total_b[...]).astype(jnp.bfloat16)
    to_swap[...] = jnp.where(first, grad_a[...], grad_b[...])
    for copy in copies:
        copy.wait()
    for out, index in ((across, 3 - g), (far, g ^ 2), (near, g ^ 1), (own, g)):
        at = pl.ds(pl.multiple_of(index * n, n), n)
        total = None
        for s, v in ((s0, v0), (sa, va), (sb, vb), (sc, vc)):
            term = jnp.dot(s[at, :], v[...], preferred_element_type=jnp.float32)
            total = term if total is None else total + term
        out[:n, :] = (scale[0] * total).astype(out.dtype)
        sums = loss[:, at]
        high = sums.astype(jnp.bfloat16).astype(jnp.float32)
        row = lax.broadcasted_iota(jnp.int32, (PAD, n), 0)
        tail = jnp.where(row == 0, high, jnp.where(row == 1, sums - high, 0.0))
        out[n:, :n] = tail.astype(out.dtype)
        out[n:, n:] = jnp.zeros((PAD, out.shape[1] - n), out.dtype)


def back_kernel(place, grad_a, grad_b, grad_c, handed_one, handed_two, by_one, by_two, by_three):
    third = place[0] == 2
    gc = grad_c[...].astype(jnp.float32)
    handed = handed_one[...].astype(jnp.float32) + handed_two[...].astype(jnp.float32)
    by_three[...] = (jnp.where(third, 0.0, gc) + handed).astype(jnp.bfloat16)
    by_two[...] = jnp.where(third, grad_c[...], grad_b[...])
    by_one[...] = grad_a[...]


def final_kernel(values, upstream, grad):
    unit, inverse = unit_rows(values)
    grad[...] = inverse * (upstream - unit * jnp.sum(unit * upstream, axis=-1, keepdims=True))


def image_final_kernel(lane, images, own, far, across, near, grad, loss_rows, values, sem):
    n = TOK_DEV
    at = pl.ds(pl.multiple_of(lane[0] * n, n), n)
    copy = pltpu.make_async_copy(images.at[at], values, sem)
    copy.start()
    parts = (own, far, across, near)
    sums = sum(p[n:, :n].astype(jnp.float32) for p in parts)
    loss_rows[...] = jnp.sum(sums, axis=0, keepdims=True) / (STEPS * TOK_DEV)
    copy.wait()
    upstream = sum(p[:n, :].astype(jnp.float32) for p in parts)
    final_kernel(values[...], upstream, grad)


def caption_final_kernel(captions, own, r3, r2, r1, grad):
    upstream = own[...] + sum(r[...].astype(jnp.float32) for r in (r1, r2, r3))
    final_kernel(captions[...], upstream, grad)


def routes(n_blk, n_group):
    def at(b, g):
        return (b % n_blk) * n_group + g

    def inside(pairs):
        return [
            (at(b + s, g), at(b + t, g))
            for b in range(0, n_blk, ROW)
            for g in range(n_group)
            for s, t in pairs
        ]

    def shift(distance):
        return inside([(s, s + distance) for s in range(ROW - distance)])

    def crossing(pairs):
        return [
            (at(b + s, g), at(b + ROW + t, n_group - 1 - g))
            for b in range(0, n_blk, ROW)
            for g in range(n_group)
            for s, t in pairs
        ]

    forward = [
        shift(3) + crossing([(ROW - 1, 1), (ROW - 2, 0)]),
        crossing([(ROW - 3, 0)]),
        shift(1),
        shift(2),
    ]
    back = [
        shift(1),
        shift(2),
        shift(3) + crossing([(ROW - 1, 1), (ROW - 2, 0), (ROW - 3, 2)]),
    ]
    return forward, back, inside([(0, 1), (1, 0)]), inside([(1, 2)]), inside([(2, 1), (0, 2)])


def body(images, captions, pairing, logit_scale, logit_bias):
    n_blk, n_group = lax.axis_size("blk"), lax.axis_size("group")
    forward, back, swap, pass_on, pass_back = routes(n_blk, n_group)
    lane = jnp.full((1,), lax.axis_index("group"), jnp.int32)
    place = jnp.full((1,), lax.axis_index("blk") % ROW, jnp.int32)
    n, width = captions.shape
    rows = images.shape[0]
    flops = 2 * rows * n * width

    def send(block, route):
        return lax.ppermute(block, AXES, route)

    def send_back(block, route):
        return lax.ppermute(block, AXES, [(t, s) for s, t in route])

    def within(block, pairs):
        return lax.ppermute(
            block, AXES, [(b * n_group + s, b * n_group + t) for b in range(n_blk) for s, t in pairs]
        )

    wide, short = jnp.float32, jnp.bfloat16
    slopes = shape((rows, n), short)
    block = shape((n, width), short)
    v0 = call(norm_kernel, block, [vmem()], 1000, "caption_unit", (captions,))
    f3, f5, f1, f2 = [send(v0, route) for route in forward]
    image_bf, loss, s0, g0 = call(
        first_kernel,
        (shape((rows, width), short), shape((1, rows), wide), slopes, shape((n, width), wide)),
        [vmem(), vmem(), vmem(), smem(), smem()],
        2 * flops,
        "first_pairs",
        (images, v0, pairing.reshape(n, 1), logit_scale, logit_bias),
        [pltpu.VMEM((n, width), wide)],
    )
    f3, loss = lax.optimization_barrier((f3, loss))
    y1 = send(f3, swap)
    y2 = send(f3, pass_on)
    loss, sc, gc, vc = call(
        next_kernel,
        (shape((1, rows), wide), slopes, block, block),
        [smem()] + [vmem()] * 4 + [smem(), smem()],
        2 * flops,
        "next_pairs",
        (place, image_bf, f2, f3, loss, logit_scale, logit_bias),
        [pltpu.VMEM((n, width), wide)],
    )
    share = shape((n + PAD, width), short)
    across, near, far, own, ga, gb, to_swap = call(
        last_kernel,
        (share, share, share, shape((n + PAD, width), wide), block, block, block),
        [smem()] * 4 + [vmem()] * 9 + [anywhere()] * 2,
        8 * flops,
        "last_pairs",
        (lane, place, logit_scale, logit_bias, image_bf, v0, f1, f2, vc, y1, y2, f5, loss, s0, sc),
        [pltpu.VMEM((rows, n), short)] * 4
        + [pltpu.VMEM((n, width), short)] * 2
        + [pltpu.VMEM((n, width), wide)] * 2
        + [pltpu.VMEM((1, rows), wide), pltpu.SemaphoreType.DMA((2,))],
    )
    y1 = send(to_swap, swap)
    y2 = send(gb, pass_back)
    far = within(far, [(0, 2), (1, 3), (2, 0), (3, 1)])
    across = within(across, [(0, 3), (1, 2), (2, 1), (3, 0)])
    near = within(near, [(0, 1), (1, 0), (2, 3), (3, 2)])
    ga, gb, gc = call(
        back_kernel,
        (block,) * 3,
        [smem()] + [vmem()] * 5,
        1000,
        "back_sums",
        (place, ga, gb, gc, y1, y2),
    )
    r3 = send_back(gc, back[2])
    r2 = send_back(gb, back[1])
    r1 = send_back(ga, back[0])
    image_grad, loss_rows = call(
        image_final_kernel,
        (shape((n, width), wide), shape((1, n), wide)),
        [smem(), anywhere()] + [vmem()] * 4,
        1000,
        "image_final",
        (lane, images, own, far, across, near),
        [pltpu.VMEM((n, width), short), pltpu.SemaphoreType.DMA],
    )
    caption_grad = call(
        caption_final_kernel,
        shape((n, width), wide),
        [vmem()] * 5,
        1000,
        "caption_final",
        (captions, g0, r3, r2, r1),
    )
    return (image_grad, caption_grad, loss_rows.reshape(n))


def solution(mesh):
    in_specs = (P("blk", None), P(("blk", "group"), None), P("blk", "group"), P(), P())
    out_specs = (P(("blk", "group"), None), P(("blk", "group"), None), P(("blk", "group")))
    return jax.shard_map(body, mesh=mesh, in_specs=in_specs, out_specs=out_specs, check_vma=False)
```

```python
import jax
import jax.numpy as jnp
from jax import lax
from jax.experimental import pallas as pl
from jax.experimental.pallas import tpu as pltpu
from jax.sharding import PartitionSpec as P

TOK_DEV = 256
STEPS = 4
AXES = ("blk", "group")
ROW = 8
PAD = 16
NEAR_FLOPS = 1 * 10**9
VMEM_BYTES = 16 * 1024 * 1024
NT = (((1,), (1,)), ((), ()))


def vmem():
    return pl.BlockSpec(memory_space=pltpu.VMEM)


def smem():
    return pl.BlockSpec(memory_space=pltpu.SMEM)


def anywhere():
    return pl.BlockSpec(memory_space=pl.ANY)


def call(kernel, outs, ins, flops, name, args, scratch=()):
    return pl.pallas_call(
        kernel,
        out_shape=outs,
        in_specs=ins,
        out_specs=jax.tree.map(lambda _: vmem(), outs),
        scratch_shapes=scratch,
        compiler_params=pltpu.CompilerParams(vmem_limit_bytes=VMEM_BYTES),
        cost_estimate=pl.CostEstimate(
            flops=flops, bytes_accessed=4 * 1024 * 1024, transcendentals=0
        ),
        name=name,
    )(*args)


def shape(dims, dtype):
    return jax.ShapeDtypeStruct(dims, dtype)


def unit_rows(values):
    as_float = values.astype(jnp.float32)
    inverse = lax.rsqrt(jnp.sum(as_float * as_float, axis=-1, keepdims=True) + 1e-06)
    return as_float * inverse, inverse


def norm_kernel(captions, out):
    out[...] = unit_rows(captions[...])[0].astype(jnp.bfloat16)


def pair_chunk(visiting, image, scale, bias, positive):
    logits = (
        scale * lax.dot_general(visiting, image, NT, preferred_element_type=jnp.float32) + bias
    )
    signed = logits if positive is None else jnp.where(positive, -logits, logits)
    small = jnp.exp(-jnp.abs(signed))
    whole = 1.0 + small
    inverse = 1.0 / whole
    log1p = jnp.log(whole) + (small - (whole - 1.0)) * inverse
    loss = jnp.sum(jnp.maximum(signed, 0.0) + log1p, axis=0, keepdims=True)
    slope = jnp.where(signed >= 0.0, inverse, small * inverse)
    if positive is not None:
        slope = jnp.where(positive, -slope, slope)
    return loss, slope


def first_kernel(images, visiting, pairing, scale, bias, image_bf, loss, slopes, grad, total):
    n, rows = TOK_DEV, image_bf.shape[0]
    held = visiting[...]
    for c in range(rows // n):
        at = slice(c * n, (c + 1) * n)
        image = unit_rows(images[at, :])[0].astype(jnp.bfloat16)
        image_bf[at, :] = image
        positive = pairing[...] == c * n + lax.broadcasted_iota(jnp.int32, (n, n), 1)
        part, slope = pair_chunk(held, image, scale[0], bias[0], positive)
        loss[:, at] = part
        slopes[at, :] = slope.T.astype(jnp.bfloat16)
        term = jnp.dot(slope.astype(jnp.bfloat16), image, preferred_element_type=jnp.float32)
        if c == 0:
            total[...] = term
        elif c < rows // n - 1:
            total[...] += term
        else:
            grad[...] = scale[0] * (total[...] + term)


def next_kernel(place, image_bf, f2, f3, before, scale, bias, loss, slopes, grad, held_out, total):
    n, rows = TOK_DEV, image_bf.shape[0]
    held = jnp.where(place[0] == 2, f2[...], f3[...])
    held_out[...] = held
    for c in range(rows // n):
        at = slice(c * n, (c + 1) * n)
        image = image_bf[at, :]
        part, slope = pair_chunk(held, image, scale[0], bias[0], None)
        loss[:, at] = before[:, at] + part
        slopes[at, :] = slope.T.astype(jnp.bfloat16)
        term = jnp.dot(slope.astype(jnp.bfloat16), image, preferred_element_type=jnp.float32)
        if c == 0:
            total[...] = term
        elif c < rows // n - 1:
            total[...] += term
        else:
            grad[...] = (scale[0] * (total[...] + term)).astype(grad.dtype)


def write_share(out, total, sums):
    n = TOK_DEV
    out[:n, :] = total.astype(out.dtype)
    high = sums.astype(jnp.bfloat16).astype(jnp.float32)
    row = lax.broadcasted_iota(jnp.int32, (PAD, n), 0)
    tail = jnp.where(row == 0, high, jnp.where(row == 1, sums - high, 0.0))
    out[n:, :n] = tail.astype(out.dtype)
    out[n:, n:] = jnp.zeros((PAD, out.shape[1] - n), out.dtype)


def rows_of(index):
    return pl.ds(pl.multiple_of(index * TOK_DEV, TOK_DEV), TOK_DEV)


def choose(held, choices):
    for chosen, source in choices:

        @pl.when(chosen)
        def _():
            held[...] = source[...]


def head_kernel(
    lane, place, scale, bias, image_bf, v0, f1, f2, vc, y1, y2, f5, before, s0_in, sc_in,
    share, va, vb, slope_a, slope_b, s0, sc, sems,
):
    p, at = place[0], rows_of(3 - lane[0])
    copies = [
        pltpu.make_async_copy(s0_in.at[at], s0, sems.at[0]),
        pltpu.make_async_copy(sc_in.at[at], sc, sems.at[1]),
    ]
    for copy in copies:
        copy.start()
    choose(va, ((p == 0, y1), (p != 0, f1)))
    choose(vb, ((p == 0, f5), (p == 1, y1), (p == 2, y2), (p > 2, f2)))
    image, sums, total = image_bf[at, :], before[:, at], None
    for v, kept in ((va, slope_a), (vb, slope_b)):
        part, slope = pair_chunk(v[...], image, scale[0], bias[0], None)
        sums = sums + part
        kept[...] = slope.astype(jnp.bfloat16)
        term = jnp.dot(slope.T.astype(jnp.bfloat16), v[...], preferred_element_type=jnp.float32)
        total = term if total is None else total + term
    for copy in copies:
        copy.wait()
    for s, v in ((s0, v0), (sc, vc)):
        total = total + jnp.dot(s[...], v[...], preferred_element_type=jnp.float32)
    write_share(share, scale[0] * total, sums)


def tail_kernel(
    lane, place, scale, bias, image_bf, v0, va, vb, vc, slope_a, slope_b, before, s0_in, sc_in,
    far, near, own, grad_a, grad_b, to_swap, s0, sc, total_a, total_b, sems,
):
    g = lane[0]
    copies = [
        pltpu.make_async_copy(s0_in, s0, sems.at[0]),
        pltpu.make_async_copy(sc_in, sc, sems.at[1]),
    ]
    for copy in copies:
        copy.start()
    image = image_bf[rows_of(3 - g), :]
    total_a[...] = jnp.dot(slope_a[...], image, preferred_element_type=jnp.float32)
    total_b[...] = jnp.dot(slope_b[...], image, preferred_element_type=jnp.float32)
    for out, index in ((far, g ^ 2), (near, g ^ 1), (own, g)):
        at = rows_of(index)
        image, sums, total = image_bf[at, :], before[:, at], None
        for v, gained in ((va, total_a), (vb, total_b)):
            part, slope = pair_chunk(v[...], image, scale[0], bias[0], None)
            sums = sums + part
            gained[...] += jnp.dot(slope.astype(jnp.bfloat16), image, preferred_element_type=jnp.float32)
            term = jnp.dot(slope.T.astype(jnp.bfloat16), v[...], preferred_element_type=jnp.float32)
            total = term if total is None else total + term
        if out is far:
            for copy in copies:
                copy.wait()
        for s, v in ((s0, v0), (sc, vc)):
            total = total + jnp.dot(s[at, :], v[...], preferred_element_type=jnp.float32)
        write_share(out, scale[0] * total, sums)
    grad_a[...] = (scale[0] * total_a[...]).astype(jnp.bfloat16)
    grad_b[...] = (scale[0] * total_b[...]).astype(jnp.bfloat16)
    to_swap[...] = jnp.where(place[0] == 0, grad_a[...], grad_b[...])


def back_kernel(place, grad_a, grad_b, grad_c, handed_one, handed_two, by_one, by_two, by_three):
    third = place[0] == 2
    gc = grad_c[...].astype(jnp.float32)
    handed = handed_one[...].astype(jnp.float32) + handed_two[...].astype(jnp.float32)
    by_three[...] = (jnp.where(third, 0.0, gc) + handed).astype(jnp.bfloat16)
    by_two[...] = jnp.where(third, grad_c[...], grad_b[...])
    by_one[...] = grad_a[...]


def sum_kernel(*refs):
    refs[-1][...] = sum(r[...].astype(jnp.float32) for r in refs[:-1]).astype(refs[-1].dtype)


def final_kernel(values, upstream, grad):
    unit, inverse = unit_rows(values)
    grad[...] = inverse * (upstream - unit * jnp.sum(unit * upstream, axis=-1, keepdims=True))


def image_final_kernel(lane, images, own, far, grad, loss_rows, values, sem):
    n = TOK_DEV
    at = pl.ds(pl.multiple_of(lane[0] * n, n), n)
    copy = pltpu.make_async_copy(images.at[at], values, sem)
    copy.start()
    parts = (own, far)
    sums = sum(p[n:, :n].astype(jnp.float32) for p in parts)
    loss_rows[...] = jnp.sum(sums, axis=0, keepdims=True) / (STEPS * TOK_DEV)
    copy.wait()
    upstream = sum(p[:n, :].astype(jnp.float32) for p in parts)
    final_kernel(values[...], upstream, grad)


def caption_final_kernel(captions, own, r3, r4, r2, r1, grad):
    upstream = own[...] + sum(r[...].astype(jnp.float32) for r in (r1, r2, r3, r4))
    final_kernel(captions[...], upstream, grad)


def routes(n_blk, n_group):
    def at(b, g):
        return (b % n_blk) * n_group + g

    def inside(pairs):
        return [
            (at(b + s, g), at(b + t, g))
            for b in range(0, n_blk, ROW)
            for g in range(n_group)
            for s, t in pairs
        ]

    def shift(distance):
        return inside([(s, s + distance) for s in range(ROW - distance)])

    def crossing(pairs):
        return [
            (at(b + s, g), at(b + ROW + t, n_group - 1 - g))
            for b in range(0, n_blk, ROW)
            for g in range(n_group)
            for s, t in pairs
        ]

    forward = [
        shift(3) + crossing([(ROW - 1, 1), (ROW - 2, 0)]),
        crossing([(ROW - 3, 0)]),
        shift(1),
        shift(2),
    ]
    back = [
        shift(1),
        shift(2),
        shift(3),
        crossing([(ROW - 1, 1), (ROW - 2, 0), (ROW - 3, 2)]),
    ]
    return forward, back, inside([(0, 1), (1, 0)]), inside([(1, 2)]), inside([(2, 1), (0, 2)])


def body(images, captions, pairing, logit_scale, logit_bias):
    n_blk, n_group = lax.axis_size("blk"), lax.axis_size("group")
    forward, back, swap, pass_on, pass_back = routes(n_blk, n_group)
    lane = jnp.full((1,), lax.axis_index("group"), jnp.int32)
    place = jnp.full((1,), lax.axis_index("blk") % ROW, jnp.int32)
    n, width = captions.shape
    rows = images.shape[0]
    flops = 2 * rows * n * width

    def send(block, route):
        return lax.ppermute(block, AXES, route)

    def send_back(block, route):
        return lax.ppermute(block, AXES, [(t, s) for s, t in route])

    def within(block, pairs):
        return lax.ppermute(
            block, AXES, [(b * n_group + s, b * n_group + t) for b in range(n_blk) for s, t in pairs]
        )

    wide, short = jnp.float32, jnp.bfloat16
    slopes = shape((rows, n), short)
    block = shape((n, width), short)
    v0 = call(norm_kernel, block, [vmem()], 1000, "caption_unit", (captions,))
    f3, f5, f1, f2 = [send(v0, route) for route in forward]
    image_bf, loss, s0, g0 = call(
        first_kernel,
        (shape((rows, width), short), shape((1, rows), wide), slopes, shape((n, width), wide)),
        [vmem(), vmem(), vmem(), smem(), smem()],
        2 * flops,
        "first_pairs",
        (images, v0, pairing.reshape(n, 1), logit_scale, logit_bias),
        [pltpu.VMEM((n, width), wide)],
    )
    f3, loss = lax.optimization_barrier((f3, loss))
    y1 = send(f3, swap)
    y2 = send(f3, pass_on)
    loss, sc, gc, vc = call(
        next_kernel,
        (shape((1, rows), wide), slopes, block, block),
        [smem()] + [vmem()] * 4 + [smem(), smem()],
        2 * flops,
        "next_pairs",
        (place, image_bf, f2, f3, loss, logit_scale, logit_bias),
        [pltpu.VMEM((n, width), wide)],
    )
    share = shape((n + PAD, width), short)
    scalars = (lane, place, logit_scale, logit_bias)
    square = shape((n, n), short)
    slope_shape = pltpu.VMEM((n, n), short)
    first_share, va, vb, slope_a, slope_b = call(
        head_kernel,
        (share, block, block, square, square),
        [smem()] * 4 + [vmem()] * 9 + [anywhere()] * 2,
        3 * flops,
        "head_pairs",
        (*scalars, image_bf, v0, f1, f2, vc, y1, y2, f5, loss, s0, sc),
        [slope_shape, slope_shape, pltpu.SemaphoreType.DMA((2,))],
    )
    far, near, own, ga, gb, to_swap = call(
        tail_kernel,
        (share, share, shape((n + PAD, width), wide), block, block, block),
        [smem()] * 4 + [vmem()] * 8 + [anywhere()] * 2,
        6 * flops,
        "tail_pairs",
        (*scalars, image_bf, v0, va, vb, vc, slope_a, slope_b, loss, s0, sc),
        [pltpu.VMEM((rows, n), short)] * 2
        + [pltpu.VMEM((n, width), wide)] * 2
        + [pltpu.SemaphoreType.DMA((2,))],
    )
    beside = [(0, 1), (1, 0), (2, 3), (3, 2)]
    halves = within(first_share, beside)
    r3 = send_back(gc, back[2])
    y1 = send(to_swap, swap)
    y2 = send(gb, pass_back)
    far, r3 = lax.optimization_barrier((far, r3))
    far = call(sum_kernel, share, [vmem()] * 2, 1000, "add_halves", (far, halves))
    far, gc = lax.optimization_barrier((far, gc))
    far = within(far, [(0, 2), (1, 3), (2, 0), (3, 1)])
    near = within(near, beside)
    ga, gb, gc = call(
        back_kernel,
        (block,) * 3,
        [smem()] + [vmem()] * 5,
        1000,
        "back_sums",
        (place, ga, gb, gc, y1, y2),
    )
    own, gc = lax.optimization_barrier((own, gc))
    own = call(
        sum_kernel, shape((n + PAD, width), wide), [vmem()] * 2, NEAR_FLOPS, "add_near", (own, near)
    )
    r4 = send_back(gc, back[3])
    r2 = send_back(gb, back[1])
    r1 = send_back(ga, back[0])
    image_grad, loss_rows = call(
        image_final_kernel,
        (shape((n, width), wide), shape((1, n), wide)),
        [smem(), anywhere()] + [vmem()] * 2,
        1000,
        "image_final",
        (lane, images, own, far),
        [pltpu.VMEM((n, width), short), pltpu.SemaphoreType.DMA],
    )
    caption_grad = call(
        caption_final_kernel,
        shape((n, width), wide),
        [vmem()] * 6,
        1000,
        "caption_final",
        (captions, g0, r3, r4, r2, r1),
    )
    return (image_grad, caption_grad, loss_rows.reshape(n))


def solution(mesh):
    in_specs = (P("blk", None), P(("blk", "group"), None), P("blk", "group"), P(), P())
    out_specs = (P(("blk", "group"), None), P(("blk", "group"), None), P(("blk", "group")))
    return jax.shard_map(body, mesh=mesh, in_specs=in_specs, out_specs=out_specs, check_vma=False)
```

```python
import jax
import jax.numpy as jnp
from jax import lax
from jax.experimental import pallas as pl
from jax.experimental.pallas import tpu as pltpu
from jax.sharding import PartitionSpec as P

TOK_DEV = 256
STEPS = 4
AXES = ("blk", "group")
ROW = 8
PAD = 16
NEAR_FLOPS = 12 * 10**9
VMEM_BYTES = 16 * 1024 * 1024
NT = (((1,), (1,)), ((), ()))


def vmem():
    return pl.BlockSpec(memory_space=pltpu.VMEM)


def smem():
    return pl.BlockSpec(memory_space=pltpu.SMEM)


def anywhere():
    return pl.BlockSpec(memory_space=pl.ANY)


def call(kernel, outs, ins, flops, name, args, scratch=()):
    return pl.pallas_call(
        kernel,
        out_shape=outs,
        in_specs=ins,
        out_specs=jax.tree.map(lambda _: vmem(), outs),
        scratch_shapes=scratch,
        compiler_params=pltpu.CompilerParams(vmem_limit_bytes=VMEM_BYTES),
        cost_estimate=pl.CostEstimate(
            flops=flops, bytes_accessed=4 * 1024 * 1024, transcendentals=0
        ),
        name=name,
    )(*args)


def shape(dims, dtype):
    return jax.ShapeDtypeStruct(dims, dtype)


def unit_rows(values):
    as_float = values.astype(jnp.float32)
    inverse = lax.rsqrt(jnp.sum(as_float * as_float, axis=-1, keepdims=True) + 1e-06)
    return as_float * inverse, inverse


def norm_kernel(captions, out):
    out[...] = unit_rows(captions[...])[0].astype(jnp.bfloat16)


def pair_chunk(visiting, image, scale, bias, positive):
    logits = (
        scale * lax.dot_general(visiting, image, NT, preferred_element_type=jnp.float32) + bias
    )
    signed = logits if positive is None else jnp.where(positive, -logits, logits)
    small = jnp.exp(-jnp.abs(signed))
    whole = 1.0 + small
    inverse = 1.0 / whole
    log1p = jnp.log(whole) + (small - (whole - 1.0)) * inverse
    loss = jnp.sum(jnp.maximum(signed, 0.0) + log1p, axis=0, keepdims=True)
    slope = jnp.where(signed >= 0.0, inverse, small * inverse)
    if positive is not None:
        slope = jnp.where(positive, -slope, slope)
    return loss, slope


def first_kernel(images, visiting, pairing, scale, bias, image_bf, loss, slopes, grad, total):
    n, rows = TOK_DEV, image_bf.shape[0]
    held = visiting[...]
    for c in range(rows // n):
        at = slice(c * n, (c + 1) * n)
        image = unit_rows(images[at, :])[0].astype(jnp.bfloat16)
        image_bf[at, :] = image
        positive = pairing[...] == c * n + lax.broadcasted_iota(jnp.int32, (n, n), 1)
        part, slope = pair_chunk(held, image, scale[0], bias[0], positive)
        loss[:, at] = part
        slopes[at, :] = slope.T.astype(jnp.bfloat16)
        term = jnp.dot(slope.astype(jnp.bfloat16), image, preferred_element_type=jnp.float32)
        if c == 0:
            total[...] = term
        elif c < rows // n - 1:
            total[...] += term
        else:
            grad[...] = scale[0] * (total[...] + term)


def next_kernel(place, image_bf, f2, f3, before, scale, bias, loss, slopes, grad, held_out, total):
    n, rows = TOK_DEV, image_bf.shape[0]
    held = jnp.where(place[0] == 2, f2[...], f3[...])
    held_out[...] = held
    for c in range(rows // n):
        at = slice(c * n, (c + 1) * n)
        image = image_bf[at, :]
        part, slope = pair_chunk(held, image, scale[0], bias[0], None)
        loss[:, at] = before[:, at] + part
        slopes[at, :] = slope.T.astype(jnp.bfloat16)
        term = jnp.dot(slope.astype(jnp.bfloat16), image, preferred_element_type=jnp.float32)
        if c == 0:
            total[...] = term
        elif c < rows // n - 1:
            total[...] += term
        else:
            grad[...] = (scale[0] * (total[...] + term)).astype(grad.dtype)


def write_share(out, total, sums):
    n = TOK_DEV
    out[:n, :] = total.astype(out.dtype)
    high = sums.astype(jnp.bfloat16).astype(jnp.float32)
    row = lax.broadcasted_iota(jnp.int32, (PAD, n), 0)
    tail = jnp.where(row == 0, high, jnp.where(row == 1, sums - high, 0.0))
    out[n:, :n] = tail.astype(out.dtype)
    out[n:, n:] = jnp.zeros((PAD, out.shape[1] - n), out.dtype)


def rows_of(index):
    return pl.ds(pl.multiple_of(index * TOK_DEV, TOK_DEV), TOK_DEV)


def choose(held, choices):
    for chosen, source in choices:

        @pl.when(chosen)
        def _():
            held[...] = source[...]


def head_kernel(
    lane, place, scale, bias, image_bf, v0, f1, f2, vc, y1, y2, f5, before, s0_in, sc_in,
    share, va, vb, slope_a, slope_b, s0, sc, sems,
):
    p, at = place[0], rows_of(3 - lane[0])
    copies = [
        pltpu.make_async_copy(s0_in.at[at], s0, sems.at[0]),
        pltpu.make_async_copy(sc_in.at[at], sc, sems.at[1]),
    ]
    for copy in copies:
        copy.start()
    choose(va, ((p == 0, y1), (p != 0, f1)))
    choose(vb, ((p == 0, f5), (p == 1, y1), (p == 2, y2), (p > 2, f2)))
    image, sums, total = image_bf[at, :], before[:, at], None
    for v, kept in ((va, slope_a), (vb, slope_b)):
        part, slope = pair_chunk(v[...], image, scale[0], bias[0], None)
        sums = sums + part
        kept[...] = slope.astype(jnp.bfloat16)
        term = jnp.dot(slope.T.astype(jnp.bfloat16), v[...], preferred_element_type=jnp.float32)
        total = term if total is None else total + term
    for copy in copies:
        copy.wait()
    for s, v in ((s0, v0), (sc, vc)):
        total = total + jnp.dot(s[...], v[...], preferred_element_type=jnp.float32)
    write_share(share, scale[0] * total, sums)


def tail_kernel(
    lane, place, scale, bias, image_bf, v0, va, vb, vc, slope_a, slope_b, before, s0_in, sc_in,
    far, near, own, grad_a, grad_b, to_swap, s0, sc, total_a, total_b, sems,
):
    g = lane[0]
    copies = [
        pltpu.make_async_copy(s0_in, s0, sems.at[0]),
        pltpu.make_async_copy(sc_in, sc, sems.at[1]),
    ]
    for copy in copies:
        copy.start()
    image = image_bf[rows_of(3 - g), :]
    total_a[...] = jnp.dot(slope_a[...], image, preferred_element_type=jnp.float32)
    total_b[...] = jnp.dot(slope_b[...], image, preferred_element_type=jnp.float32)
    for out, index in ((far, g ^ 2), (near, g ^ 1), (own, g)):
        at = rows_of(index)
        image, sums, total = image_bf[at, :], before[:, at], None
        for v, gained in ((va, total_a), (vb, total_b)):
            part, slope = pair_chunk(v[...], image, scale[0], bias[0], None)
            sums = sums + part
            gained[...] += jnp.dot(slope.astype(jnp.bfloat16), image, preferred_element_type=jnp.float32)
            term = jnp.dot(slope.T.astype(jnp.bfloat16), v[...], preferred_element_type=jnp.float32)
            total = term if total is None else total + term
        if out is far:
            for copy in copies:
                copy.wait()
        for s, v in ((s0, v0), (sc, vc)):
            total = total + jnp.dot(s[at, :], v[...], preferred_element_type=jnp.float32)
        write_share(out, scale[0] * total, sums)
    grad_a[...] = (scale[0] * total_a[...]).astype(jnp.bfloat16)
    grad_b[...] = (scale[0] * total_b[...]).astype(jnp.bfloat16)
    to_swap[...] = jnp.where(place[0] == 0, grad_a[...], grad_b[...])


def back_kernel(place, grad_a, grad_b, grad_c, handed_one, handed_two, by_one, by_two, by_three):
    third = place[0] == 2
    gc = grad_c[...].astype(jnp.float32)
    handed = handed_one[...].astype(jnp.float32) + handed_two[...].astype(jnp.float32)
    by_three[...] = (jnp.where(third, 0.0, gc) + handed).astype(jnp.bfloat16)
    by_two[...] = jnp.where(third, grad_c[...], grad_b[...])
    by_one[...] = grad_a[...]


def sum_kernel(*refs):
    refs[-1][...] = sum(r[...].astype(jnp.float32) for r in refs[:-1]).astype(refs[-1].dtype)


def final_kernel(values, upstream, grad):
    unit, inverse = unit_rows(values)
    grad[...] = inverse * (upstream - unit * jnp.sum(unit * upstream, axis=-1, keepdims=True))


def image_final_kernel(lane, images, own, far, near, grad, loss_rows, values, sem):
    n = TOK_DEV
    at = pl.ds(pl.multiple_of(lane[0] * n, n), n)
    copy = pltpu.make_async_copy(images.at[at], values, sem)
    copy.start()
    parts = (own, far, near)
    sums = sum(p[n:, :n].astype(jnp.float32) for p in parts)
    loss_rows[...] = jnp.sum(sums, axis=0, keepdims=True) / (STEPS * TOK_DEV)
    copy.wait()
    upstream = sum(p[:n, :].astype(jnp.float32) for p in parts)
    final_kernel(values[...], upstream, grad)


def caption_final_kernel(captions, own, r3, r4, r2, r1, grad):
    upstream = own[...] + sum(r[...].astype(jnp.float32) for r in (r1, r2, r3, r4))
    final_kernel(captions[...], upstream, grad)


def routes(n_blk, n_group):
    def at(b, g):
        return (b % n_blk) * n_group + g

    def inside(pairs):
        return [
            (at(b + s, g), at(b + t, g))
            for b in range(0, n_blk, ROW)
            for g in range(n_group)
            for s, t in pairs
        ]

    def shift(distance):
        return inside([(s, s + distance) for s in range(ROW - distance)])

    def crossing(pairs):
        return [
            (at(b + s, g), at(b + ROW + t, n_group - 1 - g))
            for b in range(0, n_blk, ROW)
            for g in range(n_group)
            for s, t in pairs
        ]

    forward = [
        shift(3) + crossing([(ROW - 1, 1), (ROW - 2, 0)]),
        crossing([(ROW - 3, 0)]),
        shift(1),
        shift(2),
    ]
    back = [
        shift(1),
        shift(2),
        shift(3),
        crossing([(ROW - 1, 1), (ROW - 2, 0), (ROW - 3, 2)]),
    ]
    return forward, back, inside([(0, 1), (1, 0)]), inside([(1, 2)]), inside([(2, 1), (0, 2)])


def body(images, captions, pairing, logit_scale, logit_bias):
    n_blk, n_group = lax.axis_size("blk"), lax.axis_size("group")
    forward, back, swap, pass_on, pass_back = routes(n_blk, n_group)
    lane = jnp.full((1,), lax.axis_index("group"), jnp.int32)
    place = jnp.full((1,), lax.axis_index("blk") % ROW, jnp.int32)
    n, width = captions.shape
    rows = images.shape[0]
    flops = 2 * rows * n * width

    def send(block, route):
        return lax.ppermute(block, AXES, route)

    def send_back(block, route):
        return lax.ppermute(block, AXES, [(t, s) for s, t in route])

    def within(block, pairs):
        return lax.ppermute(
            block, AXES, [(b * n_group + s, b * n_group + t) for b in range(n_blk) for s, t in pairs]
        )

    wide, short = jnp.float32, jnp.bfloat16
    slopes = shape((rows, n), short)
    block = shape((n, width), short)
    v0 = call(norm_kernel, block, [vmem()], 1000, "caption_unit", (captions,))
    f3, f5, f1, f2 = [send(v0, route) for route in forward]
    image_bf, loss, s0, g0 = call(
        first_kernel,
        (shape((rows, width), short), shape((1, rows), wide), slopes, shape((n, width), wide)),
        [vmem(), vmem(), vmem(), smem(), smem()],
        2 * flops,
        "first_pairs",
        (images, v0, pairing.reshape(n, 1), logit_scale, logit_bias),
        [pltpu.VMEM((n, width), wide)],
    )
    f3, loss = lax.optimization_barrier((f3, loss))
    y1 = send(f3, swap)
    y2 = send(f3, pass_on)
    loss, sc, gc, vc = call(
        next_kernel,
        (shape((1, rows), wide), slopes, block, block),
        [smem()] + [vmem()] * 4 + [smem(), smem()],
        2 * flops,
        "next_pairs",
        (place, image_bf, f2, f3, loss, logit_scale, logit_bias),
        [pltpu.VMEM((n, width), wide)],
    )
    share = shape((n + PAD, width), short)
    scalars = (lane, place, logit_scale, logit_bias)
    square = shape((n, n), short)
    slope_shape = pltpu.VMEM((n, n), short)
    first_share, va, vb, slope_a, slope_b = call(
        head_kernel,
        (share, block, block, square, square),
        [smem()] * 4 + [vmem()] * 9 + [anywhere()] * 2,
        3 * flops,
        "head_pairs",
        (*scalars, image_bf, v0, f1, f2, vc, y1, y2, f5, loss, s0, sc),
        [slope_shape, slope_shape, pltpu.SemaphoreType.DMA((2,))],
    )
    far, near, own, ga, gb, to_swap = call(
        tail_kernel,
        (share, share, shape((n + PAD, width), wide), block, block, block),
        [smem()] * 4 + [vmem()] * 8 + [anywhere()] * 2,
        6 * flops,
        "tail_pairs",
        (*scalars, image_bf, v0, va, vb, vc, slope_a, slope_b, loss, s0, sc),
        [pltpu.VMEM((rows, n), short)] * 2
        + [pltpu.VMEM((n, width), wide)] * 2
        + [pltpu.SemaphoreType.DMA((2,))],
    )
    beside = [(0, 1), (1, 0), (2, 3), (3, 2)]
    halves = within(first_share, beside)
    r3 = send_back(gc, back[2])
    far, r3 = lax.optimization_barrier((far, r3))
    far = call(sum_kernel, share, [vmem()] * 2, 1000, "add_halves", (far, halves))
    far, gb, gc, to_swap = lax.optimization_barrier((far, gb, gc, to_swap))
    y1 = send(to_swap, swap)
    y2 = send(gb, pass_back)
    far = within(far, [(0, 2), (1, 3), (2, 0), (3, 1)])
    near = within(near, beside)
    ga, gb, gc = call(
        back_kernel,
        (block,) * 3,
        [smem()] + [vmem()] * 5,
        1000,
        "back_sums",
        (place, ga, gb, gc, y1, y2),
    )
    r4 = send_back(gc, back[3])
    r2 = send_back(gb, back[1])
    r1 = send_back(ga, back[0])
    image_grad, loss_rows = call(
        image_final_kernel,
        (shape((n, width), wide), shape((1, n), wide)),
        [smem(), anywhere()] + [vmem()] * 3,
        NEAR_FLOPS,
        "image_final",
        (lane, images, own, far, near),
        [pltpu.VMEM((n, width), short), pltpu.SemaphoreType.DMA],
    )
    caption_grad = call(
        caption_final_kernel,
        shape((n, width), wide),
        [vmem()] * 6,
        1000,
        "caption_final",
        (captions, g0, r3, r4, r2, r1),
    )
    return (image_grad, caption_grad, loss_rows.reshape(n))


def solution(mesh):
    in_specs = (P("blk", None), P(("blk", "group"), None), P("blk", "group"), P(), P())
    out_specs = (P(("blk", "group"), None), P(("blk", "group"), None), P(("blk", "group")))
    return jax.shard_map(body, mesh=mesh, in_specs=in_specs, out_specs=out_specs, check_vma=False)
```
